256 devices in a mesh: dp: 256 (over x, y, z, core).
Axes of the slice: x: 4, y: 4, z: 8, core: 2. Of those that a mesh axis runs over, the one named last changes fastest.
Arguments:
- picture_embedding_matrix: float32 [131072, 1152], P('dp'), may hold values from -1.0298836 to 1.0298836
- caption_embedding_matrix: float32 [131072, 1152], P('dp'), may hold values from -1.0298836 to 1.0298836
- sharpness_factor: float32 [1], replicated, may hold values from 0.5 to 2
- offset_term: float32 [1], replicated, may hold values from -4 to -1
Outputs:
- picture_embedding_derivative: float32 [131072, 1152], P('dp')
- text_gradient: float32 [131072, 1152], P('dp')
The draws below stay inside these ranges and needn't reach their ends.
All inputs are finite; a program needn't handle non-finite values.
Results may differ from the reference program's by a relative error of at most 0.00011.
Values sent between devices are 32-bit elements; how exact they have to be, the bound alone decides.
A program may use at most 64 MiB of HBM per device.

```python
import math
import jax
import jax.numpy as jnp
from jax import lax

D = 1152
PAIRS = 512
STEPS = 4
BATCH = 131072
N_DP = 256


def block_scale(own_key, extent, shards, least, high):
    level = 1.0
    for dim, parts in shards:
        heights = jax.random.uniform(jax.random.fold_in(jax.random.fold_in(own_key, 6), dim), (parts,), jnp.float32, least / len(shards), high / len(shards))
        level = level * jnp.repeat(jnp.exp(heights), extent[dim] // parts).reshape((-1,) + (1,) * (len(extent) - 1 - dim))
    return level


def centred(own_key, dims, scale, bound, cuts=(), kind=jnp.bfloat16):
    gain = block_scale(own_key, dims, cuts, -0.22, 0.18) if cuts else 1.0
    entries = jax.random.normal(own_key, dims, jnp.float32) * scale * gain
    return jnp.minimum(jnp.maximum(entries, -bound), bound).astype(kind)


def setup_inputs(seed: int = 0) -> dict:
    seeds = jax.random.split(jax.random.key(seed), 5)
    picture_embedding_matrix = centred(seeds[0], (BATCH, D), (D ** -0.25), 1.0298836, ((0, 256),), jnp.float32)
    caption_embedding_matrix = centred(seeds[1], (BATCH, D), (D ** -0.25), 1.0298836, ((0, 256),), jnp.float32)
    sharpness_factor = jnp.clip(jnp.exp(jax.random.uniform(seeds[2], (1,), jnp.float32, math.log(0.5), math.log(2.0))), 0.5, 2.0)
    offset_term = jnp.clip(jax.random.uniform(seeds[3], (1,), jnp.float32, -4.0, -1.0), -4.0, -1.0)
    return dict(picture_embedding_matrix=picture_embedding_matrix, caption_embedding_matrix=caption_embedding_matrix, sharpness_factor=sharpness_factor, offset_term=offset_term)


def reference(picture_embedding_matrix, caption_embedding_matrix, sharpness_factor, offset_term):
    inverse_heat_factor = sharpness_factor[0]
    offset = offset_term[0]
    images = picture_embedding_matrix.reshape(N_DP, PAIRS, D)
    texts = caption_embedding_matrix.reshape(N_DP, PAIRS, D)
    image_acc = jnp.zeros((N_DP, PAIRS, D), jnp.float32)
    caption_derivative_running_total = jnp.zeros((N_DP, PAIRS, D), jnp.float32)
    same = jnp.eye(PAIRS, dtype=jnp.float32) > 0.5
    for step in range(STEPS):
        visit_count = jnp.roll(texts, step, axis=0)
        logits = inverse_heat_factor * jnp.einsum("npd,nqd->npq", images, visit_count, precision=lax.Precision.HIGHEST) + offset
        if step == 0:
            target_signs = jnp.where(same, 1.0, -1.0).astype(jnp.float32)
        else:
            target_signs = -jnp.ones((PAIRS, PAIRS), jnp.float32)
        slope = -target_signs * jax.nn.sigmoid(-target_signs * logits)
        image_acc = image_acc + inverse_heat_factor * jnp.einsum("npq,nqd->npd", slope, visit_count, precision=lax.Precision.HIGHEST)
        partial_text = inverse_heat_factor * jnp.einsum("npq,npd->nqd", slope, images, precision=lax.Precision.HIGHEST)
        caption_derivative_running_total = caption_derivative_running_total + jnp.roll(partial_text, -step, axis=0)
    return image_acc.reshape(BATCH, D), caption_derivative_running_total.reshape(BATCH, D)
```

```python
import functools

import jax
import jax.numpy as jnp
from jax import lax
from jax.experimental import pallas as pl
from jax.experimental.pallas import tpu as pltpu
from jax.sharding import PartitionSpec as P

MESH = pl.DeviceIdType.MESH
F32 = jnp.float32
BF16 = jnp.bfloat16

V, U, NEAR, A2, B2, PFB, PFA, Q3 = range(8)
CHUNKS = 4
HALVES = 2


def split(x):
    high = x.astype(BF16)
    return high, (x - high.astype(F32)).astype(BF16)


def dot_nt(a, b):
    return lax.dot_general(a, b, (((1,), (1,)), ((), ())), preferred_element_type=F32)


def dot_nn(a, b):
    return lax.dot_general(a, b, (((1,), (0,)), ((), ())), preferred_element_type=F32)


def kernel(n, scale_ref, offset_ref, img, txt, img_grad, txt_grad, buf, high, low, acc, load_sem, out_sem, send_sem, recv_sem):
    rows = img.shape[0]
    chunk = rows // CHUNKS
    half = rows // HALVES
    me = lax.axis_index("dp")
    odd = lax.rem(me, 2)
    e = 2 * odd - 1
    scale = scale_ref[0]
    offset = offset_ref[0]

    def device(distance):
        return (lax.rem(me + distance + n, n),)

    def by_core(do):
        @pl.when(odd == 1)
        def _():
            do(img, txt, img_grad, txt_grad)

        @pl.when(odd == 0)
        def _():
            do(txt, img, txt_grad, img_grad)

    def copy(kind, c, src, to, distance):
        part = pl.ds(c * chunk, chunk)
        return pltpu.make_async_remote_copy(
            src_ref=src.at[part],
            dst_ref=buf.at[to, part],
            send_sem=send_sem.at[kind, c],
            recv_sem=recv_sem.at[kind, c],
            device_id=device(distance),
            device_id_type=MESH,
        )

    def near(c, u):
        return copy(0, c, u, NEAR, -e)

    def a2(c, v):
        return copy(1, c, v, A2, 2 * e)

    def b2(c, u):
        return copy(2, c, u, B2, -2 * e)

    def pfb(c):
        return copy(3, c, buf.at[B2], PFB, -e)

    def pfa(c):
        return copy(4, c, buf.at[A2], PFA, -e)

    def q3(c):
        return copy(5, c, buf.at[A2], Q3, e)

    def load(u, v, *_):
        pltpu.make_async_copy(v, buf.at[V], load_sem.at[0]).start()
        pltpu.make_async_copy(u, buf.at[U], load_sem.at[1]).start()

    by_core(load)
    barrier = pltpu.get_barrier_semaphore()
    for distance in (-2, -1, 1, 2):
        pl.semaphore_signal(barrier, inc=1, device_id=device(distance), device_id_type=MESH)
    pl.semaphore_wait(barrier, 4)

    def send(u, v, *_):
        for c in range(CHUNKS):
            a2(c, v).start()
            b2(c, u).start()
        for c in range(CHUNKS):
            near(c, u).start()

    by_core(send)

    for k, block in enumerate((V, U)):
        pltpu.make_async_copy(img, buf.at[block], load_sem.at[k]).wait()
    for k, block in enumerate((U, V)):
        h, l = split(buf[block])
        high[k] = h
        low[k] = l
    acc[...] = jnp.zeros_like(acc)

    def score(block, start, size, k, diagonal):
        xh, xl = split(buf[block, pl.ds(start, size), :])
        for m in range(0, rows, 256):
            at = pl.ds(m, 256)
            ah, al = high[k, at, :], low[k, at, :]
            z = scale * (dot_nt(ah, xh) + (dot_nt(ah, xl) + dot_nt(al, xh))) + offset
            if diagonal:
                row = lax.broadcasted_iota(jnp.int32, z.shape, 0) + m
                column = lax.broadcasted_iota(jnp.int32, z.shape, 1) + start
                sign = jnp.where((row == column) & (block < NEAR), -1.0, 1.0)
                p = scale * (sign * lax.logistic(sign * z))
            else:
                p = scale * lax.logistic(z)
            ph, pl_ = split(p)
            acc[k, at, :] += dot_nn(ph, xh) + (dot_nn(ph, xl) + dot_nn(pl_, xh))

    def first(t, _):
        block = t // HALVES

        @pl.when(t == NEAR * HALVES)
        def _():
            for c in range(CHUNKS):
                near(c, img).wait_recv()

        score(block, pl.multiple_of(lax.rem(t, HALVES) * half, half), half, lax.rem(block, 2), True)
        return 0

    lax.fori_loop(0, 3 * HALVES, first, 0)

    per = CHUNKS // HALVES

    def second(t, _):
        part, which = t // 4, lax.rem(t, 4)

        @pl.when(which == 0)
        def _():
            for i in range(per):
                c = part * per + i
                a2(c, txt).wait_recv()
                pfa(c).start()
                q3(c).start()
                b2(c, img).wait_recv()
                pfb(c).start()

        @pl.when(which == 2)
        def _():
            for i in range(per):
                pfb(part * per + i).wait_recv()

        @pl.when(which == 3)
        def _():
            for i in range(per):
                pfa(part * per + i).wait_recv()

        score(A2 + which, pl.multiple_of(part * half, half), half, lax.rem(which, 2), False)
        return 0

    lax.fori_loop(0, 4 * HALVES, second, 0)

    def store(k):
        def go(img_grad, txt_grad, u_grad, v_grad):
            pltpu.make_async_copy(acc.at[k], (u_grad, v_grad)[k], out_sem.at[k]).start()

        return go

    by_core(store(0))

    def third(c, _):
        q3(c).wait_recv()
        score(Q3, pl.multiple_of(c * chunk, chunk), chunk, 1, False)
        return 0

    lax.fori_loop(0, CHUNKS, third, 0)
    by_core(store(1))
    for c in range(CHUNKS):
        near(c, img).wait_send()
        a2(c, img).wait_send()
        b2(c, img).wait_send()
        pfb(c).wait_send()
        pfa(c).wait_send()
        q3(c).wait_send()
    for k in range(2):
        pltpu.make_async_copy(acc.at[k], img_grad, out_sem.at[k]).wait()


def local(img, txt, scale, offset):
    rows, width = img.shape
    n = lax.axis_size("dp")
    hbm = pl.BlockSpec(memory_space=pltpu.HBM)
    smem = pl.BlockSpec(memory_space=pltpu.SMEM)
    return pl.pallas_call(
        functools.partial(kernel, n),
        out_shape=[jax.ShapeDtypeStruct((rows, width), F32)] * 2,
        in_specs=[smem, smem, hbm, hbm],
        out_specs=[hbm, hbm],
        scratch_shapes=[
            pltpu.VMEM((8, rows, width), F32),
            pltpu.VMEM((2, rows, width), BF16),
            pltpu.VMEM((2, rows, width), BF16),
            pltpu.VMEM((2, rows, width), F32),
            pltpu.SemaphoreType.DMA((2,)),
            pltpu.SemaphoreType.DMA((2,)),
            pltpu.SemaphoreType.DMA((6, CHUNKS)),
            pltpu.SemaphoreType.DMA((6, CHUNKS)),
        ],
        compiler_params=pltpu.CompilerParams(
            collective_id=0, has_side_effects=True, vmem_limit_bytes=52 * 2**20
        ),
    )(scale, offset, img, txt)


def solution(mesh):
    placed = (P("dp", None), P("dp", None), P(), P())
    return jax.shard_map(
        local, mesh=mesh, in_specs=placed, out_specs=(P("dp", None), P("dp", None)), check_vma=False
    )
```

```python
import functools

import jax
import jax.numpy as jnp
from jax import lax
from jax.experimental import pallas as pl
from jax.experimental.pallas import tpu as pltpu
from jax.sharding import PartitionSpec as P

MESH = pl.DeviceIdType.MESH
F32 = jnp.float32
BF16 = jnp.bfloat16
HBM = pl.BlockSpec(memory_space=pltpu.HBM)
SMEM = pl.BlockSpec(memory_space=pltpu.SMEM)
VMEM = pl.BlockSpec(memory_space=pltpu.VMEM)

V, U, NEAR, A2, B2, PFB, PFA, Q3 = range(8)
HALVES = 2
SIZES = (64,) * 8
STARTS = tuple(sum(SIZES[:i]) for i in range(len(SIZES)))
PIECES = len(SIZES)
TAIL = ((0, 256, (0, 1, 2, 3)), (256, 128, (4, 5)), (384, 64, (6,)))


def split(x):
    high = x.astype(BF16)
    return high, (x - high.astype(F32)).astype(BF16)


def dot_nt(a, b):
    return lax.dot_general(a, b, (((1,), (1,)), ((), ())), preferred_element_type=F32)


def dot_nn(a, b):
    return lax.dot_general(a, b, (((1,), (0,)), ((), ())), preferred_element_type=F32)


def similarity(ah, al, xh, xl):
    return dot_nt(ah, xh) + (dot_nt(ah, xl) + dot_nt(al, xh))


def weighted(ph, pl_, xh, xl):
    return dot_nn(ph, xh) + (dot_nn(ph, xl) + dot_nn(pl_, xh))


def weigh_small(scale, offset, ah, al, xh, xl):
    size = xh.shape[0]
    both = jnp.concatenate([xh, xl], axis=0)
    dots = dot_nt(ah, both)
    z = scale * (dots[:, :size] + (dots[:, size:] + dot_nt(al, xh))) + offset
    ph, pl_ = split(scale * lax.logistic(z))
    return dot_nn(jnp.concatenate([ph, ph, pl_], axis=1), jnp.concatenate([both, xh], axis=0))


def exchange(n, factors, img, txt, acc, high, low, tail, buf, dots, slopes, load_sem, send_sem, recv_sem):
    rows = img.shape[0]
    half = rows // HALVES
    me = lax.axis_index("dp")
    odd = lax.rem(me, 2)
    e = 2 * odd - 1

    def device(distance):
        return (lax.rem(me + distance + n, n),)

    def by_core(do):
        @pl.when(odd == 1)
        def _():
            do(img, txt)

        @pl.when(odd == 0)
        def _():
            do(txt, img)

    def copy(kind, c, src, to, distance):
        part = pl.ds(STARTS[c], SIZES[c])
        return pltpu.make_async_remote_copy(
            src_ref=src.at[part],
            dst_ref=tail if (to == Q3 and c == PIECES - 1) else buf.at[to, part],
            send_sem=send_sem.at[kind, c],
            recv_sem=recv_sem.at[kind, c],
            device_id=device(distance),
            device_id_type=MESH,
        )

    def near(u):
        return pltpu.make_async_remote_copy(
            src_ref=u,
            dst_ref=buf.at[NEAR],
            send_sem=send_sem.at[0, 0],
            recv_sem=recv_sem.at[0, 0],
            device_id=device(-e),
            device_id_type=MESH,
        )

    def a2(c, v):
        return copy(1, c, v, A2, 2 * e)

    def b2(c, u):
        return copy(2, c, u, B2, -2 * e)

    def pfb(c):
        return copy(3, c, buf.at[B2], PFB, -e)

    def pfa(c):
        return copy(4, c, buf.at[A2], PFA, -e)

    def q3(c):
        return copy(5, c, buf.at[A2], Q3, e)

    def load(u, v):
        pltpu.make_async_copy(v, buf.at[V], load_sem.at[0]).start()
        pltpu.make_async_copy(u, buf.at[U], load_sem.at[1]).start()

    by_core(load)
    barrier = pltpu.get_barrier_semaphore()
    for distance in (-2, -1, 1, 2):
        pl.semaphore_signal(barrier, inc=1, device_id=device(distance), device_id_type=MESH)
    pl.semaphore_wait(barrier, 4)

    def send(u, v):
        for c in range(PIECES):
            a2(c, v).start()
            b2(c, u).start()
        near(u).start()

    by_core(send)

    acc[...] = jnp.zeros_like(acc)
    scale = factors[0]
    offset = factors[1]
    for k, block in enumerate((V, U)):
        pltpu.make_async_copy(img, buf.at[block], load_sem.at[k]).wait()

    def own(which):
        return lax.rem(which + 1 + odd, 2)

    def prepare(t, _):
        at = pl.ds(pl.multiple_of(t * 128, 128), 128)
        for which, block in enumerate((U, V)):
            h, l = split(buf[block, at, :])
            high[own(which), at, :] = h
            low[own(which), at, :] = l
        return 0

    lax.fori_loop(0, rows // 128, prepare, 0)

    def score(block, start, size, which, diagonal):
        k = own(which)
        xh, xl = split(buf[block, pl.ds(start, size), :])
        for m in range(0, rows, 256):
            at = pl.ds(m, 256)
            dots[at, :size] = similarity(high[k, at, :], low[k, at, :], xh, xl)

        def slope(t, _):
            m = pl.multiple_of(t * 64, 64)
            at = pl.ds(m, 64)
            z = scale * dots[at, :size] + offset
            if diagonal:
                row = lax.broadcasted_iota(jnp.int32, z.shape, 0) + m
                column = lax.broadcasted_iota(jnp.int32, z.shape, 1) + start
                sign = jnp.where((row == column) & (block < NEAR), -1.0, 1.0)
                p = scale * (sign * lax.logistic(sign * z))
            else:
                p = scale * lax.logistic(z)
            ph, pl_ = split(p)
            slopes[0, at, :size] = ph
            slopes[1, at, :size] = pl_
            return 0

        lax.fori_loop(0, rows // 64, slope, 0)
        for m in range(0, rows, 256):
            at = pl.ds(m, 256)
            acc[k, at, :] += weighted(slopes[0, at, :size], slopes[1, at, :size], xh, xl)

    def score_small(block, start, size, which):
        k = own(which)
        xh, xl = split(buf[block, pl.ds(start, size), :])
        acc[k, ...] += weigh_small(scale, offset, high[k, ...], low[k, ...], xh, xl)

    def first(t, _):
        block = t // HALVES

        @pl.when(t == NEAR * HALVES)
        def _():
            near(img).wait_recv()

        score(block, pl.multiple_of(lax.rem(t, HALVES) * half, half), half, lax.rem(block, 2), True)
        return 0

    lax.fori_loop(0, 3 * HALVES, first, 0)

    def second(t, _):
        part, which = t // 4, lax.rem(t, 4)
        for h in range(HALVES):
            pieces = [c for c in range(PIECES) if STARTS[c] // half == h]

            @pl.when(t == 4 * h)
            def _():
                for c in pieces:
                    a2(c, txt).wait_recv()
                    q3(c).start()
                    pfa(c).start()
                    b2(c, img).wait_recv()
                    pfb(c).start()

            @pl.when(t == 4 * h + 2)
            def _():
                for c in pieces:
                    pfb(c).wait_recv()

            @pl.when(t == 4 * h + 3)
            def _():
                for c in pieces:
                    pfa(c).wait_recv()

        score(A2 + which, pl.multiple_of(part * half, half), half, lax.rem(which, 2), False)
        return 0

    lax.fori_loop(0, 4 * HALVES, second, 0)

    for start, size, pieces in TAIL:
        for c in pieces:
            q3(c).wait_recv()
        (score if size > 128 else score_small)(Q3, start, size, 1, *((False,) if size > 128 else ()))
    near(img).wait_send()
    for c in range(PIECES):
        a2(c, img).wait_send()
        b2(c, img).wait_send()
        pfb(c).wait_send()
        pfa(c).wait_send()
        q3(c).wait_send()
    q3(PIECES - 1).wait_recv()


def finish(factors, acc, high, low, tail, img_grad, txt_grad, result, out_sem):
    rows = high.shape[1]
    odd = lax.rem(lax.axis_index("dp"), 2)
    grads = (img_grad, txt_grad)
    scale = factors[0]
    offset = factors[1]
    done = [pltpu.make_async_copy(acc.at[k], grads[k], out_sem.at[0]) for k in range(2)]
    for k in range(2):
        pl.when(odd == 1 - k)(done[k].start)
    xh, xl = split(tail[...])
    step = 256
    for m in range(0, rows, step):
        at = pl.ds(m, step)
        result[at, :] = acc[odd, at, :] + weigh_small(scale, offset, high[odd, at, :], low[odd, at, :], xh, xl)
        for k in range(2):
            part = pltpu.make_async_copy(result.at[at], grads[k].at[at], out_sem.at[1 + m // step])
            pl.when(odd == k)(part.start)
    done[0].wait()
    for m in range(0, rows, step):
        at = pl.ds(m, step)
        pltpu.make_async_copy(result.at[at], img_grad.at[at], out_sem.at[1 + m // step]).wait()


def local(img, txt, scale, offset):
    rows, width = img.shape
    n = lax.axis_size("dp")
    factors = jnp.concatenate([scale, offset])
    img, txt = (pltpu.with_memory_space_constraint(x, pltpu.HBM) for x in (img, txt))
    kept = pl.pallas_call(
        functools.partial(exchange, n),
        out_shape=[
            pltpu.VMEM((2, rows, width), F32),
            pltpu.VMEM((2, rows, width), BF16),
            pltpu.VMEM((2, rows, width), BF16),
            pltpu.VMEM((SIZES[-1], width), F32),
        ],
        in_specs=[SMEM] + [HBM] * 2,
        out_specs=[VMEM] * 4,
        scratch_shapes=[
            pltpu.VMEM((8, rows, width), F32),
            pltpu.VMEM((rows, rows // HALVES), F32),
            pltpu.VMEM((2, rows, rows // HALVES), BF16),
            pltpu.SemaphoreType.DMA((2,)),
            pltpu.SemaphoreType.DMA((6, PIECES)),
            pltpu.SemaphoreType.DMA((6, PIECES)),
        ],
        compiler_params=pltpu.CompilerParams(collective_id=0, has_side_effects=True, vmem_limit_bytes=40 * 2**20),
    )(factors, img, txt)
    kept = [pltpu.with_memory_space_constraint(x, pltpu.VMEM) for x in kept]
    return pl.pallas_call(
        finish,
        out_shape=[jax.ShapeDtypeStruct((rows, width), F32)] * 2,
        in_specs=[SMEM] + [VMEM] * 4,
        out_specs=[HBM] * 2,
        scratch_shapes=[
            pltpu.VMEM((rows, width), F32),
            pltpu.SemaphoreType.DMA((5,)),
        ],
        compiler_params=pltpu.CompilerParams(vmem_limit_bytes=16 * 2**20),
    )(factors, *kept)


def solution(mesh):
    placed = (P("dp", None), P("dp", None), P(), P())
    return jax.shard_map(
        local, mesh=mesh, in_specs=placed, out_specs=(P("dp", None), P("dp", None)), check_vma=False
    )
```

```python
import functools

import jax
import jax.numpy as jnp
from jax import lax
from jax.experimental import pallas as pl
from jax.experimental.pallas import tpu as pltpu
from jax.sharding import PartitionSpec as P

MESH = pl.DeviceIdType.MESH
F32 = jnp.float32
BF16 = jnp.bfloat16
HBM = pl.BlockSpec(memory_space=pltpu.HBM)
SMEM = pl.BlockSpec(memory_space=pltpu.SMEM)
VMEM = pl.BlockSpec(memory_space=pltpu.VMEM)

V, U, NEAR, A2, B2, PFB, PFA, Q3 = range(8)
HALVES = 2
SIZES = (64,) * 8
STARTS = tuple(sum(SIZES[:i]) for i in range(len(SIZES)))
PIECES = len(SIZES)
TAIL = ((0, 256, (0, 1, 2, 3)), (256, 128, (4, 5)), (384, 64, (6,)))


def split(x):
    high = x.astype(BF16)
    return high, (x - high.astype(F32)).astype(BF16)


def dot_nt(a, b):
    return lax.dot_general(a, b, (((1,), (1,)), ((), ())), preferred_element_type=F32)


def dot_nn(a, b):
    return lax.dot_general(a, b, (((1,), (0,)), ((), ())), preferred_element_type=F32)


def similarity(ah, al, xh, xl):
    return dot_nt(ah, xh) + (dot_nt(ah, xl) + dot_nt(al, xh))


def weighted(ph, pl_, xh, xl):
    return dot_nn(ph, xh) + (dot_nn(ph, xl) + dot_nn(pl_, xh))


def weigh_small(scale, offset, ah, al, xh, xl):
    size = xh.shape[0]
    both = jnp.concatenate([xh, xl], axis=0)
    dots = dot_nt(ah, both)
    z = scale * (dots[:, :size] + (dots[:, size:] + dot_nt(al, xh))) + offset
    ph, pl_ = split(scale * lax.logistic(z))
    return dot_nn(jnp.concatenate([ph, ph, pl_], axis=1), jnp.concatenate([both, xh], axis=0))


def exchange(n, scale_ref, offset_ref, img, txt, acc, high, low, tail, buf, dots, slopes, entered, load_sem, send_sem, recv_sem):
    rows = img.shape[0]
    half = rows // HALVES
    me = lax.axis_index("dp")
    odd = lax.rem(me, 2)
    e = 2 * odd - 1

    def device(distance):
        return (lax.rem(me + distance + n, n),)

    def by_core(do):
        @pl.when(odd == 1)
        def _():
            do(img, txt)

        @pl.when(odd == 0)
        def _():
            do(txt, img)

    def copy(kind, c, src, to, distance):
        part = pl.ds(STARTS[c], SIZES[c])
        return pltpu.make_async_remote_copy(
            src_ref=src.at[part],
            dst_ref=tail if (to == Q3 and c == PIECES - 1) else buf.at[to, part],
            send_sem=send_sem.at[kind, c],
            recv_sem=recv_sem.at[kind, c],
            device_id=device(distance),
            device_id_type=MESH,
        )

    def near(u):
        return pltpu.make_async_remote_copy(
            src_ref=u,
            dst_ref=buf.at[NEAR],
            send_sem=send_sem.at[0, 0],
            recv_sem=recv_sem.at[0, 0],
            device_id=device(-e),
            device_id_type=MESH,
        )

    def a2(c, v):
        return copy(1, c, v, A2, 2 * e)

    def b2(c, u):
        return copy(2, c, u, B2, -2 * e)

    def pfb(c):
        return copy(3, c, buf.at[B2], PFB, -e)

    def pfa(c):
        return copy(4, c, buf.at[A2], PFA, -e)

    def q3(c):
        return copy(5, c, buf.at[A2], Q3, e)

    def load(u, v):
        pltpu.make_async_copy(v, buf.at[V], load_sem.at[0]).start()
        pltpu.make_async_copy(u, buf.at[U], load_sem.at[1]).start()

    barrier = pltpu.get_barrier_semaphore()
    for distance in (-2, -1):
        pl.semaphore_signal(barrier, inc=1, device_id=device(distance), device_id_type=MESH)
    by_core(load)
    pl.semaphore_wait(barrier, 2)
    for i in range(2):
        pl.semaphore_signal(entered.at[i], inc=1, device_id=device(i + 1), device_id_type=MESH)

    def send(u, v, upper):
        for c in range(PIECES):
            (a2(c, v) if upper else b2(c, u)).start()

    pl.when(odd == 1)(lambda: send(img, txt, True))
    pl.when(odd == 0)(lambda: send(txt, img, False))
    for i in range(2):
        pl.semaphore_wait(entered.at[i], 1)
    pl.when(odd == 1)(lambda: send(img, txt, False))
    pl.when(odd == 0)(lambda: send(txt, img, True))
    by_core(lambda u, v: near(u).start())

    acc[...] = jnp.zeros_like(acc)
    scale = scale_ref[0]
    offset = offset_ref[0]
    for k, block in enumerate((V, U)):
        pltpu.make_async_copy(img, buf.at[block], load_sem.at[k]).wait()

    def own(which):
        return lax.rem(which + 1 + odd, 2)

    def prepare(t, _):
        at = pl.ds(pl.multiple_of(t * 128, 128), 128)
        for which, block in enumerate((U, V)):
            h, l = split(buf[block, at, :])
            high[own(which), at, :] = h
            low[own(which), at, :] = l
        return 0

    lax.fori_loop(0, rows // 128, prepare, 0)

    def score(block, start, size, which, diagonal):
        k = own(which)
        xh, xl = split(buf[block, pl.ds(start, size), :])
        for m in range(0, rows, 256):
            at = pl.ds(m, 256)
            dots[at, :size] = similarity(high[k, at, :], low[k, at, :], xh, xl)

        def slope(t, _):
            m = pl.multiple_of(t * 64, 64)
            at = pl.ds(m, 64)
            z = scale * dots[at, :size] + offset
            if diagonal:
                row = lax.broadcasted_iota(jnp.int32, z.shape, 0) + m
                column = lax.broadcasted_iota(jnp.int32, z.shape, 1) + start
                sign = jnp.where((row == column) & (block < NEAR), -1.0, 1.0)
                p = scale * (sign * lax.logistic(sign * z))
            else:
                p = scale * lax.logistic(z)
            ph, pl_ = split(p)
            slopes[0, at, :size] = ph
            slopes[1, at, :size] = pl_
            return 0

        lax.fori_loop(0, rows // 64, slope, 0)
        for m in range(0, rows, 256):
            at = pl.ds(m, 256)
            acc[k, at, :] += weighted(slopes[0, at, :size], slopes[1, at, :size], xh, xl)

    def score_small(block, start, size, which):
        k = own(which)
        xh, xl = split(buf[block, pl.ds(start, size), :])
        acc[k, ...] += weigh_small(scale, offset, high[k, ...], low[k, ...], xh, xl)

    def first(t, _):
        block = t // HALVES

        @pl.when(t == NEAR * HALVES)
        def _():
            near(img).wait_recv()

        score(block, pl.multiple_of(lax.rem(t, HALVES) * half, half), half, lax.rem(block, 2), True)
        return 0

    lax.fori_loop(0, 3 * HALVES, first, 0)

    def second(t, _):
        part, which = t // 4, lax.rem(t, 4)
        for h in range(HALVES):
            pieces = [c for c in range(PIECES) if STARTS[c] // half == h]

            @pl.when(t == 4 * h)
            def _():
                for c in pieces:
                    a2(c, txt).wait_recv()
                    q3(c).start()
                    pfa(c).start()
                    b2(c, img).wait_recv()
                    pfb(c).start()

            @pl.when(t == 4 * h + 2)
            def _():
                for c in pieces:
                    pfb(c).wait_recv()

            @pl.when(t == 4 * h + 3)
            def _():
                for c in pieces:
                    pfa(c).wait_recv()

        score(A2 + which, pl.multiple_of(part * half, half), half, lax.rem(which, 2), False)
        return 0

    lax.fori_loop(0, 4 * HALVES, second, 0)

    for start, size, pieces in TAIL:
        for c in pieces:
            q3(c).wait_recv()
        (score if size > 128 else score_small)(Q3, start, size, 1, *((False,) if size > 128 else ()))
    near(img).wait_send()
    for c in range(PIECES):
        a2(c, img).wait_send()
        b2(c, img).wait_send()
        pfb(c).wait_send()
        pfa(c).wait_send()
        q3(c).wait_send()
    q3(PIECES - 1).wait_recv()


def finish(scale_ref, offset_ref, acc, high, low, tail, img_grad, txt_grad, result, out_sem):
    rows = high.shape[1]
    odd = lax.rem(lax.axis_index("dp"), 2)
    grads = (img_grad, txt_grad)
    scale = scale_ref[0]
    offset = offset_ref[0]
    done = [pltpu.make_async_copy(acc.at[k], grads[k], out_sem.at[0]) for k in range(2)]
    for k in range(2):
        pl.when(odd == 1 - k)(done[k].start)
    xh, xl = split(tail[...])
    step = 256
    for m in range(0, rows, step):
        at = pl.ds(m, step)
        result[at, :] = acc[odd, at, :] + weigh_small(scale, offset, high[odd, at, :], low[odd, at, :], xh, xl)
        for k in range(2):
            part = pltpu.make_async_copy(result.at[at], grads[k].at[at], out_sem.at[1 + m // step])
            pl.when(odd == k)(part.start)
    done[0].wait()
    for m in range(0, rows, step):
        at = pl.ds(m, step)
        pltpu.make_async_copy(result.at[at], img_grad.at[at], out_sem.at[1 + m // step]).wait()


def local(img, txt, scale, offset):
    rows, width = img.shape
    n = lax.axis_size("dp")
    img, txt = (pltpu.with_memory_space_constraint(x, pltpu.HBM) for x in (img, txt))
    kept = pl.pallas_call(
        functools.partial(exchange, n),
        out_shape=[
            pltpu.VMEM((2, rows, width), F32),
            pltpu.VMEM((2, rows, width), BF16),
            pltpu.VMEM((2, rows, width), BF16),
            pltpu.VMEM((SIZES[-1], width), F32),
        ],
        in_specs=[SMEM] * 2 + [HBM] * 2,
        out_specs=[VMEM] * 4,
        scratch_shapes=[
            pltpu.VMEM((8, rows, width), F32),
            pltpu.VMEM((rows, rows // HALVES), F32),
            pltpu.VMEM((2, rows, rows // HALVES), BF16),
            pltpu.SemaphoreType.REGULAR((2,)),
            pltpu.SemaphoreType.DMA((2,)),
            pltpu.SemaphoreType.DMA((6, PIECES)),
            pltpu.SemaphoreType.DMA((6, PIECES)),
        ],
        compiler_params=pltpu.CompilerParams(collective_id=0, has_side_effects=True, vmem_limit_bytes=40 * 2**20),
    )(scale, offset, img, txt)
    kept = [pltpu.with_memory_space_constraint(x, pltpu.VMEM) for x in kept]
    return pl.pallas_call(
        finish,
        out_shape=[jax.ShapeDtypeStruct((rows, width), F32)] * 2,
        in_specs=[SMEM] * 2 + [VMEM] * 4,
        out_specs=[HBM] * 2,
        scratch_shapes=[
            pltpu.VMEM((rows, width), F32),
            pltpu.SemaphoreType.DMA((5,)),
        ],
        compiler_params=pltpu.CompilerParams(vmem_limit_bytes=16 * 2**20),
    )(scale, offset, *kept)


def solution(mesh):
    placed = (P("dp", None), P("dp", None), P(), P())
    return jax.shard_map(
        local, mesh=mesh, in_specs=placed, out_specs=(P("dp", None), P("dp", None)), check_vma=False
    )
```

```python
import functools

import jax
import jax.numpy as jnp
from jax import lax
from jax.experimental import pallas as pl
from jax.experimental.pallas import tpu as pltpu
from jax.sharding import PartitionSpec as P

MESH = pl.DeviceIdType.MESH
F32 = jnp.float32
BF16 = jnp.bfloat16
HBM = pl.BlockSpec(memory_space=pltpu.HBM)
SMEM = pl.BlockSpec(memory_space=pltpu.SMEM)
VMEM = pl.BlockSpec(memory_space=pltpu.VMEM)

V, U, NEAR, A2, B2, PFB, PFA, Q3 = range(8)
HALVES = 2
LINE = 8
LINES = 4
SIZES = (64, 64, 64, 64, 64, 64, 80, 48)
PART = SIZES[-1] // 2
STARTS = tuple(sum(SIZES[:i]) for i in range(len(SIZES)))
PIECES = len(SIZES)
TAIL = ((0, 256, (0, 1, 2, 3)), (256, 128, (4, 5)), (384, 80, (6,)))


def split(x):
    high = x.astype(BF16)
    return high, (x - high.astype(F32)).astype(BF16)


def dot_nt(a, b):
    return lax.dot_general(a, b, (((1,), (1,)), ((), ())), preferred_element_type=F32)


def dot_nn(a, b):
    return lax.dot_general(a, b, (((1,), (0,)), ((), ())), preferred_element_type=F32)


def similarity(ah, al, xh, xl):
    return dot_nt(ah, xh) + (dot_nt(ah, xl) + dot_nt(al, xh))


def weighted(ph, pl_, xh, xl):
    return dot_nn(ph, xh) + (dot_nn(ph, xl) + dot_nn(pl_, xh))


def weigh_small(scale, offset, ah, al, xh, xl):
    size = xh.shape[0]
    both = jnp.concatenate([xh, xl], axis=0)
    dots = dot_nt(ah, both)
    z = scale * (dots[:, :size] + (dots[:, size:] + dot_nt(al, xh))) + offset
    ph, pl_ = split(scale * lax.logistic(z))
    return dot_nn(jnp.concatenate([ph, ph, pl_], axis=1), jnp.concatenate([both, xh], axis=0))


def exchange(n, scale_ref, offset_ref, img, txt, acc, high, low, tail, buf, dots, slopes, parked, entered, load_sem, send_sem, recv_sem, aside_send, parked_sem, passed_send, passed_recv, onward_send, onward_recv):
    rows = img.shape[0]
    half = rows // HALVES
    me = lax.axis_index("dp")
    odd = lax.rem(me, 2)
    e = 2 * odd - 1

    def device(distance):
        return (lax.rem(me + distance + n, n),)

    def by_core(do):
        @pl.when(odd == 1)
        def _():
            do(img, txt)

        @pl.when(odd == 0)
        def _():
            do(txt, img)

    def copy(kind, c, src, to, distance):
        part = pl.ds(STARTS[c], SIZES[c])
        return pltpu.make_async_remote_copy(
            src_ref=src.at[part],
            dst_ref=tail if (to == Q3 and c == PIECES - 1) else buf.at[to, part],
            send_sem=send_sem.at[kind, c],
            recv_sem=recv_sem.at[kind, c],
            device_id=device(distance),
            device_id_type=MESH,
        )

    def near(u):
        return pltpu.make_async_remote_copy(
            src_ref=u,
            dst_ref=buf.at[NEAR],
            send_sem=send_sem.at[0, 0],
            recv_sem=recv_sem.at[0, 0],
            device_id=device(-e),
            device_id_type=MESH,
        )

    def a2(c, v):
        return copy(1, c, v, A2, 2 * e)

    def b2(c, u):
        return copy(2, c, u, B2, -2 * e)

    def pfb(c):
        return copy(3, c, buf.at[B2], PFB, -e)

    def pfa(c):
        return copy(4, c, buf.at[A2], PFA, -e)

    def q3(c):
        return copy(5, c, buf.at[A2], Q3, e)

    def aside():
        return pltpu.make_async_remote_copy(
            src_ref=txt.at[pl.ds(STARTS[-1], SIZES[-1])],
            dst_ref=parked,
            send_sem=aside_send,
            recv_sem=parked_sem,
            device_id=device(-(LINES - 1) * 2 * LINE),
            device_id_type=MESH,
        )

    def passed():
        return pltpu.make_async_remote_copy(
            src_ref=parked.at[pl.ds(PART, PART)],
            dst_ref=parked.at[pl.ds(PART, PART)],
            send_sem=passed_send,
            recv_sem=passed_recv,
            device_id=device(2 * LINE),
            device_id_type=MESH,
        )

    def onward(k):
        return pltpu.make_async_remote_copy(
            src_ref=parked.at[pl.ds(k * PART, PART)],
            dst_ref=buf.at[B2, pl.ds(STARTS[-1] + k * PART, PART)],
            send_sem=onward_send.at[k],
            recv_sem=onward_recv.at[k],
            device_id=device(2 + (LINES - 1 - k) * 2 * LINE),
            device_id_type=MESH,
        )

    def load(u, v):
        pltpu.make_async_copy(v, buf.at[V], load_sem.at[0]).start()
        pltpu.make_async_copy(u, buf.at[U], load_sem.at[1]).start()

    z = lax.rem(me // 2, LINE)
    first, last = z == 0, z == LINE - 1
    above_early, below_early = z >= LINE - 2, (z >= 1) & (z <= LINE - 2)
    one = lambda condition: condition.astype(jnp.int32)
    is_odd, is_even = odd == 1, odd == 0
    y = lax.rem(me // (2 * LINE), LINES)
    detoured = is_even & last & (y == LINES - 1)
    helper = is_even & last & (y == 0)
    second_helper = is_even & last & (y == 1)
    relieved = is_even & first & (y == 0)

    def tell(semaphore, distance):
        pl.semaphore_signal(semaphore, inc=1, device_id=device(distance), device_id_type=MESH)

    def when(condition, do):
        pl.when(condition)(do)

    barrier = pltpu.get_barrier_semaphore()

    @pl.when(first | last)
    def _():
        tell(barrier, -2)
        when(is_even, lambda: tell(barrier, -1))

    @pl.when(z < LINE - 2)
    def _():
        tell(barrier, 2)
        when(is_odd, lambda: tell(barrier, 1))

    when(is_odd & (z != LINE - 1), lambda: tell(barrier, -1))

    @pl.when(relieved)
    def _():
        for k in range(2):
            tell(barrier, -2 - (LINES - 1 - k) * 2 * LINE)

    when(helper, lambda: tell(barrier, (LINES - 1) * 2 * LINE))
    from_below, from_above, from_core = one(below_early), one(above_early), one(z != LINE - 1)
    signals = (1 - odd) * (from_core + 2 * from_below + from_above) + odd * (from_below + 2 * from_above)
    signals += one(helper | second_helper | detoured)
    when(signals > 0, lambda: pl.semaphore_wait(barrier, signals))

    def send(u, v, upper):
        for c in range(PIECES - 1):
            (a2(c, v) if upper else b2(c, u)).start()
        if upper:
            a2(PIECES - 1, v).start()
        else:
            pl.when(jnp.logical_not(detoured))(b2(PIECES - 1, u).start)

    def send_up():
        pl.when(is_odd)(lambda: send(img, txt, True))
        pl.when(is_even)(lambda: send(txt, img, False))

    def send_down():
        pl.when(is_odd)(lambda: send(img, txt, False))
        pl.when(is_even)(lambda: send(txt, img, True))

    @pl.when(above_early)
    def _():
        tell(entered.at[1], 2)
        when(is_odd, lambda: tell(entered.at[1], 1))
        pl.when(detoured)(aside().start)
        send_up()

    @pl.when(below_early)
    def _():
        tell(entered.at[0], -2)
        when(is_even, lambda: tell(entered.at[0], -1))
        send_down()

    when(is_even & (z != LINE - 1), lambda: tell(entered.at[2], 1))
    by_core(load)
    when(helper, lambda: tell(entered.at[3], 2 + (LINES - 1) * 2 * LINE))
    when(second_helper, lambda: tell(entered.at[3], 2 + (LINES - 2) * 2 * LINE))
    @pl.when(z < LINE - 2)
    def _():
        pl.semaphore_wait(entered.at[0], 1 + odd)
        send_up()

    @pl.when(last)
    def _():
        pl.semaphore_wait(entered.at[1], 2 - odd)
        send_down()

    when(is_odd | last, lambda: pl.semaphore_wait(entered.at[2], 1))
    by_core(lambda u, v: near(u).start())

    @pl.when(first)
    def _():
        pl.semaphore_wait(entered.at[1], 2 - odd)
        send_down()

        @pl.when(is_even)
        def _():
            tell(entered.at[2], -1)
            tell(entered.at[2], -2)

        @pl.when(relieved)
        def _():
            pl.semaphore_wait(entered.at[3], 2)
            tell(entered.at[3], -2 - (LINES - 1) * 2 * LINE)

    acc[...] = jnp.zeros_like(acc)
    scale = scale_ref[0]
    offset = offset_ref[0]
    for k, block in enumerate((V, U)):
        pltpu.make_async_copy(img, buf.at[block], load_sem.at[k]).wait()

    def own(which):
        return lax.rem(which + 1 + odd, 2)

    def prepare(t, _):
        at = pl.ds(pl.multiple_of(t * 128, 128), 128)
        for which, block in enumerate((U, V)):
            h, l = split(buf[block, at, :])
            high[own(which), at, :] = h
            low[own(which), at, :] = l
        return 0

    lax.fori_loop(0, rows // 128, prepare, 0)

    def score(block, start, size, which, diagonal):
        k = own(which)
        xh, xl = split(buf[block, pl.ds(start, size), :])
        for m in range(0, rows, 256):
            at = pl.ds(m, 256)
            dots[at, :size] = similarity(high[k, at, :], low[k, at, :], xh, xl)

        def slope(t, _):
            m = pl.multiple_of(t * 64, 64)
            at = pl.ds(m, 64)
            z = scale * dots[at, :size] + offset
            if diagonal:
                row = lax.broadcasted_iota(jnp.int32, z.shape, 0) + m
                column = lax.broadcasted_iota(jnp.int32, z.shape, 1) + start
                sign = jnp.where((row == column) & (block < NEAR), -1.0, 1.0)
                p = scale * (sign * lax.logistic(sign * z))
            else:
                p = scale * lax.logistic(z)
            ph, pl_ = split(p)
            slopes[0, at, :size] = ph
            slopes[1, at, :size] = pl_
            return 0

        lax.fori_loop(0, rows // 64, slope, 0)
        for m in range(0, rows, 256):
            at = pl.ds(m, 256)
            acc[k, at, :] += weighted(slopes[0, at, :size], slopes[1, at, :size], xh, xl)

    def score_small(block, start, size, which):
        k = own(which)
        xh, xl = split(buf[block, pl.ds(start, size), :])
        acc[k, ...] += weigh_small(scale, offset, high[k, ...], low[k, ...], xh, xl)

    def first(t, _):
        block = t // HALVES

        @pl.when(t == NEAR * HALVES)
        def _():
            near(img).wait_recv()

        score(block, pl.multiple_of(lax.rem(t, HALVES) * half, half), half, lax.rem(block, 2), True)
        return 0

    lax.fori_loop(0, 3 * HALVES, first, 0)

    def second(t, _):
        part, which = t // 4, lax.rem(t, 4)
        for h in range(HALVES):
            pieces = [c for c in range(PIECES) if STARTS[c] // half == h]

            @pl.when(t == 4 * h)
            def _():
                if h == 0:

                    @pl.when(helper)
                    def _():
                        aside().wait_recv()
                        onward(0).start()
                        pl.semaphore_wait(entered.at[3], 1)
                        passed().start()

                for c in pieces:
                    a2(c, txt).wait_recv()
                    q3(c).start()
                    pfa(c).start()
                    if c < PIECES - 1:
                        b2(c, img).wait_recv()
                    else:
                        pl.when(jnp.logical_not(relieved))(b2(c, img).wait_recv)

                        @pl.when(relieved)
                        def _():
                            for k in range(2):
                                onward(k).wait_recv()

                    pfb(c).start()

            @pl.when(t == 4 * h + 2)
            def _():
                if h == 0:

                    @pl.when(second_helper)
                    def _():
                        passed().wait_recv()
                        onward(1).start()

                for c in pieces:
                    pfb(c).wait_recv()

            @pl.when(t == 4 * h + 3)
            def _():
                for c in pieces:
                    pfa(c).wait_recv()

        score(A2 + which, pl.multiple_of(part * half, half), half, lax.rem(which, 2), False)
        return 0

    lax.fori_loop(0, 4 * HALVES, second, 0)

    for start, size, pieces in TAIL:
        for c in pieces:
            q3(c).wait_recv()
        (score if size > 128 else score_small)(Q3, start, size, 1, *((False,) if size > 128 else ()))
    near(img).wait_send()
    for c in range(PIECES):
        a2(c, img).wait_send()
        if c < PIECES - 1:
            b2(c, img).wait_send()
        pfb(c).wait_send()
        pfa(c).wait_send()
        q3(c).wait_send()
    pl.when(jnp.logical_not(detoured))(b2(PIECES - 1, img).wait_send)
    pl.when(detoured)(aside().wait_send)

    @pl.when(helper)
    def _():
        onward(0).wait_send()
        passed().wait_send()

    pl.when(second_helper)(onward(1).wait_send)
    q3(PIECES - 1).wait_recv()


def finish(scale_ref, offset_ref, acc, high, low, tail, img_grad, txt_grad, result, out_sem):
    rows = high.shape[1]
    odd = lax.rem(lax.axis_index("dp"), 2)
    grads = (img_grad, txt_grad)
    scale = scale_ref[0]
    offset = offset_ref[0]
    done = [pltpu.make_async_copy(acc.at[k], grads[k], out_sem.at[0]) for k in range(2)]
    for k in range(2):
        pl.when(odd == 1 - k)(done[k].start)
    xh, xl = split(tail[...])
    step = 256
    for m in range(0, rows, step):
        at = pl.ds(m, step)
        result[at, :] = acc[odd, at, :] + weigh_small(scale, offset, high[odd, at, :], low[odd, at, :], xh, xl)
        for k in range(2):
            part = pltpu.make_async_copy(result.at[at], grads[k].at[at], out_sem.at[1 + m // step])
            pl.when(odd == k)(part.start)
    done[0].wait()
    for m in range(0, rows, step):
        at = pl.ds(m, step)
        pltpu.make_async_copy(result.at[at], img_grad.at[at], out_sem.at[1 + m // step]).wait()


def local(img, txt, scale, offset):
    rows, width = img.shape
    n = lax.axis_size("dp")
    img, txt = (pltpu.with_memory_space_constraint(x, pltpu.HBM) for x in (img, txt))
    kept = pl.pallas_call(
        functools.partial(exchange, n),
        out_shape=[
            pltpu.VMEM((2, rows, width), F32),
            pltpu.VMEM((2, rows, width), BF16),
            pltpu.VMEM((2, rows, width), BF16),
            pltpu.VMEM((SIZES[-1], width), F32),
        ],
        in_specs=[SMEM] * 2 + [HBM] * 2,
        out_specs=[VMEM] * 4,
        scratch_shapes=[
            pltpu.VMEM((8, rows, width), F32),
            pltpu.VMEM((rows, rows // HALVES), F32),
            pltpu.VMEM((2, rows, rows // HALVES), BF16),
            pltpu.VMEM((SIZES[-1], width), F32),
            pltpu.SemaphoreType.REGULAR((4,)),
            pltpu.SemaphoreType.DMA((2,)),
            pltpu.SemaphoreType.DMA((6, PIECES)),
            pltpu.SemaphoreType.DMA((6, PIECES)),
            pltpu.SemaphoreType.DMA,
            pltpu.SemaphoreType.DMA,
            pltpu.SemaphoreType.DMA,
            pltpu.SemaphoreType.DMA,
            pltpu.SemaphoreType.DMA((2,)),
            pltpu.SemaphoreType.DMA((2,)),
        ],
        compiler_params=pltpu.CompilerParams(collective_id=0, has_side_effects=True, vmem_limit_bytes=40 * 2**20),
    )(scale, offset, img, txt)
    kept = [pltpu.with_memory_space_constraint(x, pltpu.VMEM) for x in kept]
    return pl.pallas_call(
        finish,
        out_shape=[jax.ShapeDtypeStruct((rows, width), F32)] * 2,
        in_specs=[SMEM] * 2 + [VMEM] * 4,
        out_specs=[HBM] * 2,
        scratch_shapes=[
            pltpu.VMEM((rows, width), F32),
            pltpu.SemaphoreType.DMA((5,)),
        ],
        compiler_params=pltpu.CompilerParams(vmem_limit_bytes=16 * 2**20),
    )(scale, offset, *kept)


def solution(mesh):
    placed = (P("dp", None), P("dp", None), P(), P())
    return jax.shard_map(
        local, mesh=mesh, in_specs=placed, out_specs=(P("dp", None), P("dp", None)), check_vma=False
    )
```

```python
import functools

import jax
import jax.numpy as jnp
from jax import lax
from jax.experimental import pallas as pl
from jax.experimental.pallas import tpu as pltpu
from jax.sharding import PartitionSpec as P

MESH = pl.DeviceIdType.MESH
F32 = jnp.float32
BF16 = jnp.bfloat16
HBM = pl.BlockSpec(memory_space=pltpu.HBM)
SMEM = pl.BlockSpec(memory_space=pltpu.SMEM)
VMEM = pl.BlockSpec(memory_space=pltpu.VMEM)

V, U, NEAR, A2, B2, PFB, PFA, Q3 = range(8)
HALVES = 2
LINE = 8
LINES = 4
SIZES = (64, 64, 64, 64, 64, 64, 80, 48)
PART = SIZES[-1] // 2
STARTS = tuple(sum(SIZES[:i]) for i in range(len(SIZES)))
PIECES = len(SIZES)
TAIL = ((0, 256, (0, 1, 2, 3)), (256, 128, (4, 5)), (384, 80, (6,)))


def split(x):
    high = x.astype(BF16)
    return high, (x - high.astype(F32)).astype(BF16)


def dot_nt(a, b):
    return lax.dot_general(a, b, (((1,), (1,)), ((), ())), preferred_element_type=F32)


def dot_nn(a, b):
    return lax.dot_general(a, b, (((1,), (0,)), ((), ())), preferred_element_type=F32)


def similarity(ah, al, xh, xl):
    return dot_nt(ah, xh) + (dot_nt(ah, xl) + dot_nt(al, xh))


def weighted(ph, pl_, xh, xl):
    return dot_nn(ph, xh) + (dot_nn(ph, xl) + dot_nn(pl_, xh))


def weigh_small(scale, offset, ah, al, xh, xl):
    size = xh.shape[0]
    both = jnp.concatenate([xh, xl], axis=0)
    dots = dot_nt(ah, both)
    z = scale * (dots[:, :size] + (dots[:, size:] + dot_nt(al, xh))) + offset
    ph, pl_ = split(scale * lax.logistic(z))
    return dot_nn(jnp.concatenate([ph, ph, pl_], axis=1), jnp.concatenate([both, xh], axis=0))


def exchange(n, scale_ref, offset_ref, img, txt, acc, high, low, tail, buf, dots, slopes, parked, entered, load_sem, send_sem, recv_sem, aside_send, parked_sem, passed_send, passed_recv, onward_send, onward_recv):
    rows = img.shape[0]
    half = rows // HALVES
    me = lax.axis_index("dp")
    odd = lax.rem(me, 2)
    e = 2 * odd - 1

    def device(distance):
        return (lax.rem(me + distance + n, n),)

    def by_core(do):
        @pl.when(odd == 1)
        def _():
            do(img, txt)

        @pl.when(odd == 0)
        def _():
            do(txt, img)

    def copy(kind, c, src, to, distance):
        part = pl.ds(STARTS[c], SIZES[c])
        return pltpu.make_async_remote_copy(
            src_ref=src.at[part],
            dst_ref=tail if (to == Q3 and c == PIECES - 1) else buf.at[to, part],
            send_sem=send_sem.at[kind, c],
            recv_sem=recv_sem.at[kind, c],
            device_id=device(distance),
            device_id_type=MESH,
        )

    def near(u):
        return pltpu.make_async_remote_copy(
            src_ref=u,
            dst_ref=buf.at[NEAR],
            send_sem=send_sem.at[0, 0],
            recv_sem=recv_sem.at[0, 0],
            device_id=device(-e),
            device_id_type=MESH,
        )

    def a2(c, v):
        return copy(1, c, v, A2, 2 * e)

    def b2(c, u):
        return copy(2, c, u, B2, -2 * e)

    def pfb(c):
        return copy(3, c, buf.at[B2], PFB, -e)

    def pfa(c):
        return copy(4, c, buf.at[A2], PFA, -e)

    def q3(c):
        return copy(5, c, buf.at[A2], Q3, e)

    def aside(u):
        return pltpu.make_async_remote_copy(
            src_ref=u.at[pl.ds(STARTS[-1], SIZES[-1])],
            dst_ref=parked,
            send_sem=aside_send,
            recv_sem=parked_sem,
            device_id=device(-sign * (LINES - 1) * 2 * LINE),
            device_id_type=MESH,
        )

    def passed():
        return pltpu.make_async_remote_copy(
            src_ref=parked.at[pl.ds(PART, PART)],
            dst_ref=parked.at[pl.ds(PART, PART)],
            send_sem=passed_send,
            recv_sem=passed_recv,
            device_id=device(sign * 2 * LINE),
            device_id_type=MESH,
        )

    def onward(k):
        return pltpu.make_async_remote_copy(
            src_ref=parked.at[pl.ds(k * PART, PART)],
            dst_ref=buf.at[B2, pl.ds(STARTS[-1] + k * PART, PART)],
            send_sem=onward_send.at[k],
            recv_sem=onward_recv.at[k],
            device_id=device(sign * (2 + (LINES - 1 - k) * 2 * LINE)),
            device_id_type=MESH,
        )

    def load(u, v):
        pltpu.make_async_copy(v, buf.at[V], load_sem.at[0]).start()
        pltpu.make_async_copy(u, buf.at[U], load_sem.at[1]).start()

    z = lax.rem(me // 2, LINE)
    first, last = z == 0, z == LINE - 1
    above_early, below_early = z >= LINE - 2, (z >= 1) & (z <= LINE - 2)
    one = lambda condition: condition.astype(jnp.int32)
    is_odd, is_even = odd == 1, odd == 0
    y = lax.rem(me // (2 * LINE), LINES)
    sign = 1 - 2 * odd

    def at(end_of_even, y_of_even):
        return (is_even & end_of_even & (y == y_of_even)) | (is_odd & (last if end_of_even is first else first) & (y == LINES - 1 - y_of_even))

    detoured, helper, second_helper, relieved = at(last, LINES - 1), at(last, 0), at(last, 1), at(first, 0)

    def tell(semaphore, distance):
        pl.semaphore_signal(semaphore, inc=1, device_id=device(distance), device_id_type=MESH)

    def when(condition, do):
        pl.when(condition)(do)

    barrier = pltpu.get_barrier_semaphore()

    @pl.when(first | last)
    def _():
        tell(barrier, -2)
        when(is_even, lambda: tell(barrier, -1))

    @pl.when(z < LINE - 2)
    def _():
        tell(barrier, 2)
        when(is_odd, lambda: tell(barrier, 1))

    when(is_odd & (z != LINE - 1), lambda: tell(barrier, -1))

    @pl.when(relieved & is_even)
    def _():
        for k in range(2):
            tell(barrier, -2 - (LINES - 1 - k) * 2 * LINE)

    for k, role in enumerate((helper, second_helper)):
        when(role & is_odd, lambda: tell(barrier, -2 - (LINES - 1 - k) * 2 * LINE))
    when(helper, lambda: tell(barrier, sign * (LINES - 1) * 2 * LINE))
    from_below, from_above, from_core = one(below_early), one(above_early), one(z != LINE - 1)
    signals = (1 - odd) * (from_core + 2 * from_below + from_above) + odd * (from_below + 2 * from_above)
    signals += one(detoured) + (1 - odd) * one(helper | second_helper) + 2 * odd * one(relieved)
    when(signals > 0, lambda: pl.semaphore_wait(barrier, signals))

    def send(u, v, upper):
        for c in range(PIECES - 1):
            (a2(c, v) if upper else b2(c, u)).start()
        if upper:
            a2(PIECES - 1, v).start()
        else:
            pl.when(jnp.logical_not(detoured))(b2(PIECES - 1, u).start)

    def send_up():
        pl.when(is_odd)(lambda: send(img, txt, True))
        pl.when(is_even)(lambda: send(txt, img, False))

    def send_down():
        pl.when(is_odd)(lambda: send(img, txt, False))
        pl.when(is_even)(lambda: send(txt, img, True))

    @pl.when(above_early)
    def _():
        tell(entered.at[1], 2)
        when(is_odd, lambda: tell(entered.at[1], 1))
        pl.when(detoured & is_even)(aside(txt).start)
        send_up()

    @pl.when(below_early)
    def _():
        tell(entered.at[0], -2)
        when(is_even, lambda: tell(entered.at[0], -1))
        send_down()

    when(is_even & (z != LINE - 1), lambda: tell(entered.at[2], 1))
    by_core(load)
    pl.when(detoured & is_odd)(aside(img).start)
    for k, role in enumerate((helper, second_helper)):
        when(role & is_even, lambda: tell(entered.at[3], 2 + (LINES - 1 - k) * 2 * LINE))
        when(relieved & is_odd, lambda: tell(entered.at[3], 2 + (LINES - 1 - k) * 2 * LINE))
    @pl.when(z < LINE - 2)
    def _():
        pl.semaphore_wait(entered.at[0], 1 + odd)
        send_up()

    @pl.when(last)
    def _():
        pl.semaphore_wait(entered.at[1], 2 - odd)
        send_down()

    when(is_odd | last, lambda: pl.semaphore_wait(entered.at[2], 1))
    by_core(lambda u, v: near(u).start())

    @pl.when(first)
    def _():
        pl.semaphore_wait(entered.at[1], 2 - odd)
        send_down()

        @pl.when(is_even)
        def _():
            tell(entered.at[2], -1)
            tell(entered.at[2], -2)

        @pl.when(relieved)
        def _():
            pl.semaphore_wait(entered.at[3], 2)
            tell(entered.at[3], -2 - (LINES - 1) * 2 * LINE)

    acc[...] = jnp.zeros_like(acc)
    scale = scale_ref[0]
    offset = offset_ref[0]
    for k, block in enumerate((V, U)):
        pltpu.make_async_copy(img, buf.at[block], load_sem.at[k]).wait()

    def own(which):
        return lax.rem(which + 1 + odd, 2)

    def prepare(t, _):
        at = pl.ds(pl.multiple_of(t * 128, 128), 128)
        for which, block in enumerate((U, V)):
            h, l = split(buf[block, at, :])
            high[own(which), at, :] = h
            low[own(which), at, :] = l
        return 0

    lax.fori_loop(0, rows // 128, prepare, 0)

    def score(block, start, size, which, diagonal):
        k = own(which)
        xh, xl = split(buf[block, pl.ds(start, size), :])
        for m in range(0, rows, 256):
            at = pl.ds(m, 256)
            dots[at, :size] = similarity(high[k, at, :], low[k, at, :], xh, xl)

        def slope(t, _):
            m = pl.multiple_of(t * 64, 64)
            at = pl.ds(m, 64)
            z = scale * dots[at, :size] + offset
            if diagonal:
                row = lax.broadcasted_iota(jnp.int32, z.shape, 0) + m
                column = lax.broadcasted_iota(jnp.int32, z.shape, 1) + start
                sign = jnp.where((row == column) & (block < NEAR), -1.0, 1.0)
                p = scale * (sign * lax.logistic(sign * z))
            else:
                p = scale * lax.logistic(z)
            ph, pl_ = split(p)
            slopes[0, at, :size] = ph
            slopes[1, at, :size] = pl_
            return 0

        lax.fori_loop(0, rows // 64, slope, 0)
        for m in range(0, rows, 256):
            at = pl.ds(m, 256)
            acc[k, at, :] += weighted(slopes[0, at, :size], slopes[1, at, :size], xh, xl)

    def score_small(block, start, size, which):
        k = own(which)
        xh, xl = split(buf[block, pl.ds(start, size), :])
        acc[k, ...] += weigh_small(scale, offset, high[k, ...], low[k, ...], xh, xl)

    def first(t, _):
        block = t // HALVES

        @pl.when(t == NEAR * HALVES)
        def _():
            near(img).wait_recv()

        score(block, pl.multiple_of(lax.rem(t, HALVES) * half, half), half, lax.rem(block, 2), True)
        return 0

    lax.fori_loop(0, 3 * HALVES, first, 0)

    def second(t, _):
        part, which = t // 4, lax.rem(t, 4)
        for h in range(HALVES):
            pieces = [c for c in range(PIECES) if STARTS[c] // half == h]

            @pl.when(t == 4 * h)
            def _():
                if h == 0:

                    @pl.when(helper)
                    def _():
                        aside(img).wait_recv()
                        pl.semaphore_wait(entered.at[3], 1)
                        onward(0).start()
                        passed().start()

                for c in pieces:
                    a2(c, txt).wait_recv()
                    q3(c).start()
                    pfa(c).start()
                    if c < PIECES - 1:
                        b2(c, img).wait_recv()
                    else:
                        pl.when(jnp.logical_not(relieved))(b2(c, img).wait_recv)

                        @pl.when(relieved)
                        def _():
                            for k in range(2):
                                onward(k).wait_recv()

                    pfb(c).start()

            @pl.when(t == 4 * h + 2)
            def _():
                if h == 0:

                    @pl.when(second_helper)
                    def _():
                        passed().wait_recv()
                        when(is_odd, lambda: pl.semaphore_wait(entered.at[3], 1))
                        onward(1).start()

                for c in pieces:
                    pfb(c).wait_recv()

            @pl.when(t == 4 * h + 3)
            def _():
                for c in pieces:
                    pfa(c).wait_recv()

        score(A2 + which, pl.multiple_of(part * half, half), half, lax.rem(which, 2), False)
        return 0

    lax.fori_loop(0, 4 * HALVES, second, 0)

    for start, size, pieces in TAIL:
        for c in pieces:
            q3(c).wait_recv()
        (score if size > 128 else score_small)(Q3, start, size, 1, *((False,) if size > 128 else ()))
    near(img).wait_send()
    for c in range(PIECES):
        a2(c, img).wait_send()
        if c < PIECES - 1:
            b2(c, img).wait_send()
        pfb(c).wait_send()
        pfa(c).wait_send()
        q3(c).wait_send()
    pl.when(jnp.logical_not(detoured))(b2(PIECES - 1, img).wait_send)
    pl.when(detoured)(aside(img).wait_send)

    @pl.when(helper)
    def _():
        onward(0).wait_send()
        passed().wait_send()

    pl.when(second_helper)(onward(1).wait_send)
    q3(PIECES - 1).wait_recv()


def finish(scale_ref, offset_ref, acc, high, low, tail, img_grad, txt_grad, result, out_sem):
    rows = high.shape[1]
    odd = lax.rem(lax.axis_index("dp"), 2)
    grads = (img_grad, txt_grad)
    scale = scale_ref[0]
    offset = offset_ref[0]
    done = [pltpu.make_async_copy(acc.at[k], grads[k], out_sem.at[0]) for k in range(2)]
    for k in range(2):
        pl.when(odd == 1 - k)(done[k].start)
    xh, xl = split(tail[...])
    step = 256
    for m in range(0, rows, step):
        at = pl.ds(m, step)
        result[at, :] = acc[odd, at, :] + weigh_small(scale, offset, high[odd, at, :], low[odd, at, :], xh, xl)
        for k in range(2):
            part = pltpu.make_async_copy(result.at[at], grads[k].at[at], out_sem.at[1 + m // step])
            pl.when(odd == k)(part.start)
    done[0].wait()
    for m in range(0, rows, step):
        at = pl.ds(m, step)
        pltpu.make_async_copy(result.at[at], img_grad.at[at], out_sem.at[1 + m // step]).wait()


def local(img, txt, scale, offset):
    rows, width = img.shape
    n = lax.axis_size("dp")
    img, txt = (pltpu.with_memory_space_constraint(x, pltpu.HBM) for x in (img, txt))
    kept = pl.pallas_call(
        functools.partial(exchange, n),
        out_shape=[
            pltpu.VMEM((2, rows, width), F32),
            pltpu.VMEM((2, rows, width), BF16),
            pltpu.VMEM((2, rows, width), BF16),
            pltpu.VMEM((SIZES[-1], width), F32),
        ],
        in_specs=[SMEM] * 2 + [HBM] * 2,
        out_specs=[VMEM] * 4,
        scratch_shapes=[
            pltpu.VMEM((8, rows, width), F32),
            pltpu.VMEM((rows, rows // HALVES), F32),
            pltpu.VMEM((2, rows, rows // HALVES), BF16),
            pltpu.VMEM((SIZES[-1], width), F32),
            pltpu.SemaphoreType.REGULAR((4,)),
            pltpu.SemaphoreType.DMA((2,)),
            pltpu.SemaphoreType.DMA((6, PIECES)),
            pltpu.SemaphoreType.DMA((6, PIECES)),
            pltpu.SemaphoreType.DMA,
            pltpu.SemaphoreType.DMA,
            pltpu.SemaphoreType.DMA,
            pltpu.SemaphoreType.DMA,
            pltpu.SemaphoreType.DMA((2,)),
            pltpu.SemaphoreType.DMA((2,)),
        ],
        compiler_params=pltpu.CompilerParams(collective_id=0, has_side_effects=True, vmem_limit_bytes=40 * 2**20),
    )(scale, offset, img, txt)
    kept = [pltpu.with_memory_space_constraint(x, pltpu.VMEM) for x in kept]
    return pl.pallas_call(
        finish,
        out_shape=[jax.ShapeDtypeStruct((rows, width), F32)] * 2,
        in_specs=[SMEM] * 2 + [VMEM] * 4,
        out_specs=[HBM] * 2,
        scratch_shapes=[
            pltpu.VMEM((rows, width), F32),
            pltpu.SemaphoreType.DMA((5,)),
        ],
        compiler_params=pltpu.CompilerParams(vmem_limit_bytes=16 * 2**20),
    )(scale, offset, *kept)


def solution(mesh):
    placed = (P("dp", None), P("dp", None), P(), P())
    return jax.shard_map(
        local, mesh=mesh, in_specs=placed, out_specs=(P("dp", None), P("dp", None)), check_vma=False
    )
```

```python
import functools

import jax
import jax.numpy as jnp
from jax import lax
from jax.experimental import pallas as pl
from jax.experimental.pallas import tpu as pltpu
from jax.sharding import PartitionSpec as P

MESH = pl.DeviceIdType.MESH
F32 = jnp.float32
BF16 = jnp.bfloat16
HBM = pl.BlockSpec(memory_space=pltpu.HBM)
SMEM = pl.BlockSpec(memory_space=pltpu.SMEM)
VMEM = pl.BlockSpec(memory_space=pltpu.VMEM)

V, U, NEAR, A2, B2, PFB, PFA, Q3 = range(8)
HALVES = 2
LINE = 8
LINES = 4
SIZES = (64, 64, 64, 64, 64, 64, 80, 48)
PART = SIZES[-1] // 2
STARTS = tuple(sum(SIZES[:i]) for i in range(len(SIZES)))
PIECES = len(SIZES)
TAIL = ((0, 256, (0, 1, 2, 3)), (256, 128, (4, 5)), (384, 80, (6,)))


def split(x):
    high = x.astype(BF16)
    return high, (x - high.astype(F32)).astype(BF16)


def dot_nt(a, b):
    return lax.dot_general(a, b, (((1,), (1,)), ((), ())), preferred_element_type=F32)


def dot_nn(a, b):
    return lax.dot_general(a, b, (((1,), (0,)), ((), ())), preferred_element_type=F32)


def similarity(ah, al, xh, xl):
    return dot_nt(ah, xh) + (dot_nt(ah, xl) + dot_nt(al, xh))


def weighted(ph, pl_, xh, xl):
    return dot_nn(ph, xh) + (dot_nn(ph, xl) + dot_nn(pl_, xh))


def weigh_small(scale, offset, ah, al, xh, xl):
    size = xh.shape[0]
    both = jnp.concatenate([xh, xl], axis=0)
    dots = dot_nt(ah, both)
    z = scale * (dots[:, :size] + (dots[:, size:] + dot_nt(al, xh))) + offset
    ph, pl_ = split(scale * lax.logistic(z))
    return dot_nn(jnp.concatenate([ph, ph, pl_], axis=1), jnp.concatenate([both, xh], axis=0))


def exchange(n, scale_ref, offset_ref, img, txt, acc, high, low, tail, buf, dots, slopes, parked, entered, load_sem, send_sem, recv_sem, aside_send, parked_sem, passed_send, passed_recv, onward_send, onward_recv):
    rows = img.shape[0]
    half = rows // HALVES
    me = lax.axis_index("dp")
    odd = lax.rem(me, 2)
    e = 2 * odd - 1

    def device(distance):
        return (lax.rem(me + distance + n, n),)

    def by_core(do):
        @pl.when(odd == 1)
        def _():
            do(img, txt)

        @pl.when(odd == 0)
        def _():
            do(txt, img)

    def copy(kind, c, src, to, distance):
        part = pl.ds(STARTS[c], SIZES[c])
        return pltpu.make_async_remote_copy(
            src_ref=src.at[part],
            dst_ref=tail if (to == Q3 and c == PIECES - 1) else buf.at[to, part],
            send_sem=send_sem.at[kind, c],
            recv_sem=recv_sem.at[kind, c],
            device_id=device(distance),
            device_id_type=MESH,
        )

    def near(u):
        return pltpu.make_async_remote_copy(
            src_ref=u,
            dst_ref=buf.at[NEAR],
            send_sem=send_sem.at[0, 0],
            recv_sem=recv_sem.at[0, 0],
            device_id=device(-e),
            device_id_type=MESH,
        )

    def a2(c, v):
        return copy(1, c, v, A2, 2 * e)

    def b2(c, u):
        return copy(2, c, u, B2, -2 * e)

    def pfb(c):
        return copy(3, c, buf.at[B2], PFB, -e)

    def pfa(c):
        return copy(4, c, buf.at[A2], PFA, -e)

    def q3(c):
        return copy(5, c, buf.at[A2], Q3, e)

    def aside(u):
        return pltpu.make_async_remote_copy(
            src_ref=u.at[pl.ds(STARTS[-1], SIZES[-1])],
            dst_ref=parked,
            send_sem=aside_send,
            recv_sem=parked_sem,
            device_id=device(-sign * (LINES - 1) * 2 * LINE),
            device_id_type=MESH,
        )

    def passed():
        return pltpu.make_async_remote_copy(
            src_ref=parked.at[pl.ds(PART, PART)],
            dst_ref=parked.at[pl.ds(PART, PART)],
            send_sem=passed_send,
            recv_sem=passed_recv,
            device_id=device(sign * 2 * LINE),
            device_id_type=MESH,
        )

    def onward(k):
        return pltpu.make_async_remote_copy(
            src_ref=parked.at[pl.ds(k * PART, PART)],
            dst_ref=buf.at[B2, pl.ds(STARTS[-1] + k * PART, PART)],
            send_sem=onward_send.at[k],
            recv_sem=onward_recv.at[k],
            device_id=device(sign * (2 + (LINES - 1 - k) * 2 * LINE)),
            device_id_type=MESH,
        )

    def load(u, v):
        pltpu.make_async_copy(v, buf.at[V], load_sem.at[0]).start()
        pltpu.make_async_copy(u, buf.at[U], load_sem.at[1]).start()

    z = lax.rem(me // 2, LINE)
    first, last = z == 0, z == LINE - 1
    above_early, below_early = z >= LINE - 2, (z >= 1) & (z <= LINE - 2)
    one = lambda condition: condition.astype(jnp.int32)
    is_odd, is_even = odd == 1, odd == 0
    y = lax.rem(me // (2 * LINE), LINES)
    sign = 1 - 2 * odd

    def at(end_of_even, y_of_even):
        return (is_even & end_of_even & (y == y_of_even)) | (is_odd & (last if end_of_even is first else first) & (y == LINES - 1 - y_of_even))

    detoured, helper, second_helper, relieved = at(last, LINES - 1), at(last, 0), at(last, 1), at(first, 0)

    def tell(semaphore, distance):
        pl.semaphore_signal(semaphore, inc=1, device_id=device(distance), device_id_type=MESH)

    def when(condition, do):
        pl.when(condition)(do)

    barrier = pltpu.get_barrier_semaphore()

    @pl.when(first | last)
    def _():
        tell(barrier, -2)
        when(is_even, lambda: tell(barrier, -1))

    @pl.when(z < LINE - 2)
    def _():
        tell(barrier, 2)
        when(is_odd, lambda: tell(barrier, 1))

    when(is_odd & (z != LINE - 1), lambda: tell(barrier, -1))

    @pl.when(relieved & is_even)
    def _():
        for k in range(2):
            tell(barrier, -2 - (LINES - 1 - k) * 2 * LINE)

    for k, role in enumerate((helper, second_helper)):
        when(role & is_odd, lambda: tell(barrier, -2 - (LINES - 1 - k) * 2 * LINE))
    when(helper, lambda: tell(barrier, sign * (LINES - 1) * 2 * LINE))
    from_below, from_above, from_core = one(below_early), one(above_early), one(z != LINE - 1)
    signals = (1 - odd) * (from_core + 2 * from_below + from_above) + odd * (from_below + 2 * from_above)
    signals += one(detoured) + (1 - odd) * one(helper | second_helper) + 2 * odd * one(relieved)
    when(signals > 0, lambda: pl.semaphore_wait(barrier, signals))

    def send(u, v, upper):
        for c in range(PIECES - 1):
            (a2(c, v) if upper else b2(c, u)).start()
        if upper:
            a2(PIECES - 1, v).start()
        else:
            pl.when(jnp.logical_not(detoured))(b2(PIECES - 1, u).start)

    def send_up():
        pl.when(is_odd)(lambda: send(img, txt, True))
        pl.when(is_even)(lambda: send(txt, img, False))

    def send_down():
        pl.when(is_odd)(lambda: send(img, txt, False))
        pl.when(is_even)(lambda: send(txt, img, True))

    @pl.when(above_early)
    def _():
        tell(entered.at[1], 2)
        when(is_odd, lambda: tell(entered.at[1], 1))
        pl.when(detoured & is_even)(aside(txt).start)
        send_up()

    @pl.when(below_early)
    def _():
        tell(entered.at[0], -2)
        when(is_even, lambda: tell(entered.at[0], -1))
        send_down()

    when(is_even & (z != LINE - 1), lambda: tell(entered.at[2], 1))
    by_core(load)
    pl.when(detoured & is_odd)(aside(img).start)
    for k, role in enumerate((helper, second_helper)):
        when(role & is_even, lambda: tell(entered.at[3], 2 + (LINES - 1 - k) * 2 * LINE))
        when(relieved & is_odd, lambda: tell(entered.at[3], 2 + (LINES - 1 - k) * 2 * LINE))
    @pl.when(z < LINE - 2)
    def _():
        pl.semaphore_wait(entered.at[0], 1 + odd)
        send_up()

    @pl.when(last)
    def _():
        pl.semaphore_wait(entered.at[1], 2 - odd)
        send_down()

    when(is_odd | last, lambda: pl.semaphore_wait(entered.at[2], 1))
    by_core(lambda u, v: near(u).start())

    @pl.when(first)
    def _():
        pl.semaphore_wait(entered.at[1], 2 - odd)
        send_down()

        @pl.when(is_even)
        def _():
            tell(entered.at[2], -1)
            tell(entered.at[2], -2)

        @pl.when(relieved)
        def _():
            pl.semaphore_wait(entered.at[3], 2)
            tell(entered.at[3], -2 - (LINES - 1) * 2 * LINE)

    acc[...] = jnp.zeros_like(acc)
    scale = scale_ref[0]
    offset = offset_ref[0]
    for k, block in enumerate((V, U)):
        pltpu.make_async_copy(img, buf.at[block], load_sem.at[k]).wait()

    def own(which):
        return lax.rem(which + 1 + odd, 2)

    def prepare(t, _):
        at = pl.ds(pl.multiple_of(t * 128, 128), 128)
        for which, block in enumerate((U, V)):
            h, l = split(buf[block, at, :])
            high[own(which), at, :] = h
            low[own(which), at, :] = l
        return 0

    lax.fori_loop(0, rows // 128, prepare, 0)

    def score(block, start, size, which, diagonal):
        k = own(which)
        xh, xl = split(buf[block, pl.ds(start, size), :])
        for m in range(0, rows, 256):
            at = pl.ds(m, 256)
            dots[at, :size] = similarity(high[k, at, :], low[k, at, :], xh, xl)

        def slope(t, _):
            m = pl.multiple_of(t * 64, 64)
            at = pl.ds(m, 64)
            z = scale * dots[at, :size] + offset
            if diagonal:
                row = lax.broadcasted_iota(jnp.int32, z.shape, 0) + m
                column = lax.broadcasted_iota(jnp.int32, z.shape, 1) + start
                sign = jnp.where((row == column) & (block < NEAR), -1.0, 1.0)
                p = scale * (sign * lax.logistic(sign * z))
            else:
                p = scale * lax.logistic(z)
            ph, pl_ = split(p)
            slopes[0, at, :size] = ph
            slopes[1, at, :size] = pl_
            return 0

        lax.fori_loop(0, rows // 64, slope, 0)
        for m in range(0, rows, 256):
            at = pl.ds(m, 256)
            acc[k, at, :] += weighted(slopes[0, at, :size], slopes[1, at, :size], xh, xl)

    def score_small(block, start, size, which):
        k = own(which)
        xh, xl = split(buf[block, pl.ds(start, size), :])
        acc[k, ...] += weigh_small(scale, offset, high[k, ...], low[k, ...], xh, xl)

    def first(t, _):
        block = t // HALVES

        @pl.when(t == NEAR * HALVES)
        def _():
            near(img).wait_recv()

        score(block, pl.multiple_of(lax.rem(t, HALVES) * half, half), half, lax.rem(block, 2), True)
        return 0

    lax.fori_loop(0, 3 * HALVES, first, 0)

    def second(t, _):
        part, which = t // 4, lax.rem(t, 4)
        for h in range(HALVES):
            pieces = [c for c in range(PIECES) if STARTS[c] // half == h]

            @pl.when(t == 4 * h)
            def _():
                if h == 0:

                    @pl.when(helper)
                    def _():
                        aside(img).wait_recv()
                        pl.semaphore_wait(entered.at[3], 1)
                        onward(0).start()
                        passed().start()

                for c in pieces:
                    a2(c, txt).wait_recv()
                    q3(c).start()
                    pfa(c).start()
                    if c < PIECES - 1:
                        b2(c, img).wait_recv()
                    else:
                        pl.when(jnp.logical_not(relieved))(b2(c, img).wait_recv)

                        @pl.when(relieved)
                        def _():
                            for k in range(2):
                                onward(k).wait_recv()

                    pfb(c).start()

            @pl.when(t == 4 * h + 2)
            def _():
                if h == 0:

                    @pl.when(second_helper)
                    def _():
                        passed().wait_recv()
                        when(is_odd, lambda: pl.semaphore_wait(entered.at[3], 1))
                        onward(1).start()

                for c in pieces:
                    pfb(c).wait_recv()

            @pl.when(t == 4 * h + 3)
            def _():
                for c in pieces:
                    pfa(c).wait_recv()

        score(A2 + which, pl.multiple_of(part * half, half), half, lax.rem(which, 2), False)
        return 0

    lax.fori_loop(0, 4 * HALVES, second, 0)

    near(img).wait_send()
    for c in range(PIECES):
        a2(c, img).wait_send()
        if c < PIECES - 1:
            b2(c, img).wait_send()
        pfb(c).wait_send()
        pfa(c).wait_send()
    pl.when(jnp.logical_not(detoured))(b2(PIECES - 1, img).wait_send)
    pl.when(detoured)(aside(img).wait_send)

    @pl.when(helper)
    def _():
        onward(0).wait_send()
        passed().wait_send()

    pl.when(second_helper)(onward(1).wait_send)
    for start, size, pieces in TAIL:
        for c in pieces:
            q3(c).wait_recv()
        (score if size > 128 else score_small)(Q3, start, size, 1, *((False,) if size > 128 else ()))
    for c in range(PIECES):
        q3(c).wait_send()
    q3(PIECES - 1).wait_recv()


def finish(scale_ref, offset_ref, acc, high, low, tail, img_grad, txt_grad, result, out_sem):
    rows = high.shape[1]
    odd = lax.rem(lax.axis_index("dp"), 2)
    grads = (img_grad, txt_grad)
    scale = scale_ref[0]
    offset = offset_ref[0]
    done = [pltpu.make_async_copy(acc.at[k], grads[k], out_sem.at[0]) for k in range(2)]
    for k in range(2):
        pl.when(odd == 1 - k)(done[k].start)
    xh, xl = split(tail[...])
    tiles = ((0, 384), (384, 128))
    for i, (m, step) in enumerate(tiles):
        at = pl.ds(m, step)
        result[at, :] = acc[odd, at, :] + weigh_small(scale, offset, high[odd, at, :], low[odd, at, :], xh, xl)
        for k in range(2):
            part = pltpu.make_async_copy(result.at[at], grads[k].at[at], out_sem.at[1 + i])
            pl.when(odd == k)(part.start)
    done[0].wait()
    for i, (m, step) in enumerate(tiles):
        at = pl.ds(m, step)
        pltpu.make_async_copy(result.at[at], img_grad.at[at], out_sem.at[1 + i]).wait()


def local(img, txt, scale, offset):
    rows, width = img.shape
    n = lax.axis_size("dp")
    img, txt = (pltpu.with_memory_space_constraint(x, pltpu.HBM) for x in (img, txt))
    kept = pl.pallas_call(
        functools.partial(exchange, n),
        out_shape=[
            pltpu.VMEM((2, rows, width), F32),
            pltpu.VMEM((2, rows, width), BF16),
            pltpu.VMEM((2, rows, width), BF16),
            pltpu.VMEM((SIZES[-1], width), F32),
        ],
        in_specs=[SMEM] * 2 + [HBM] * 2,
        out_specs=[VMEM] * 4,
        scratch_shapes=[
            pltpu.VMEM((8, rows, width), F32),
            pltpu.VMEM((rows, rows // HALVES), F32),
            pltpu.VMEM((2, rows, rows // HALVES), BF16),
            pltpu.VMEM((SIZES[-1], width), F32),
            pltpu.SemaphoreType.REGULAR((4,)),
            pltpu.SemaphoreType.DMA((2,)),
            pltpu.SemaphoreType.DMA((6, PIECES)),
            pltpu.SemaphoreType.DMA((6, PIECES)),
            pltpu.SemaphoreType.DMA,
            pltpu.SemaphoreType.DMA,
            pltpu.SemaphoreType.DMA,
            pltpu.SemaphoreType.DMA,
            pltpu.SemaphoreType.DMA((2,)),
            pltpu.SemaphoreType.DMA((2,)),
        ],
        compiler_params=pltpu.CompilerParams(collective_id=0, has_side_effects=True, vmem_limit_bytes=40 * 2**20),
    )(scale, offset, img, txt)
    kept = [pltpu.with_memory_space_constraint(x, pltpu.VMEM) for x in kept]
    return pl.pallas_call(
        finish,
        out_shape=[jax.ShapeDtypeStruct((rows, width), F32)] * 2,
        in_specs=[SMEM] * 2 + [VMEM] * 4,
        out_specs=[HBM] * 2,
        scratch_shapes=[
            pltpu.VMEM((rows, width), F32),
            pltpu.SemaphoreType.DMA((5,)),
        ],
        compiler_params=pltpu.CompilerParams(vmem_limit_bytes=16 * 2**20),
    )(scale, offset, *kept)


def solution(mesh):
    placed = (P("dp", None), P("dp", None), P(), P())
    return jax.shard_map(
        local, mesh=mesh, in_specs=placed, out_specs=(P("dp", None), P("dp", None)), check_vma=False
    )
```
